512 devices in a mesh: member: 16 (over z, core), cell: 32 (over y, x).
Axes of the slice: x: 4, y: 8, z: 8, core: 2. Of those that a mesh axis runs over, the one named last changes fastest.
Arguments:
- preds: bfloat16 [16, 100, 32768], P('member', None, 'cell'), may hold values from -6 to 6
- target: bfloat16 [100, 32768], P(None, 'cell'), may hold values from -6 to 6
- area: float32 [32768], P('cell'), may hold values from 0.1 to 1
- channel_weight: float32 [100], replicated, may hold values from 0.1 to 1
- neighbours: int32 [4, 32768], P(None, 'cell'), may hold values from 0 to 32767, as said below
Outputs:
- losses: float32 [4], replicated
- grad: float32 [16, 100, 32768], P('member', None, 'cell')
The draws below stay inside these ranges and needn't reach their ends.
Inputs may be any that keep to these rules, and one draw needn't show every extreme that they name: Each neighbour lies within 720 cells of its cell; neighbours[0] is 720 cells before and neighbours[1] 720 cells after, clipped to the grid.
All inputs are finite; a program needn't handle non-finite values.
Results may differ from the reference program's by a relative error of at most 0.0004.
Values sent between devices are 32-bit elements; how exact they have to be, the bound alone decides.
No kernel may reach another device: no remote copies, remote signals or barrier semaphores. Data moves between devices by JAX's collectives and lax.ppermute only.
A program may use at most 64 MiB of HBM per device.

```python
import math
import jax
import jax.numpy as jnp
from jax import lax

M = 16
C = 100
ROW = 720
NEIGH = 4
CELLS = 32768


def draw_neighbours(key, part):
    key = jax.random.fold_in(key, 7)
    positions = jnp.arange(CELLS, dtype=jnp.int32)
    offsets = jax.random.randint(key, (2, CELLS), -ROW, ROW + 1, dtype=jnp.int32)
    stacked = jnp.stack([positions - ROW, positions + ROW, positions + offsets[0], positions + offsets[1]])
    return jnp.clip(stacked, 0, CELLS - 1).astype(jnp.int32)


def steps_of(key, shape, split, smallest, largest):
    def one(position, shards_of):
        heights = jax.random.uniform(jax.random.fold_in(jax.random.fold_in(key, 6), position), (shards_of,), jnp.float32, smallest / len(split), largest / len(split))
        return jnp.repeat(jnp.exp(heights), shape[position] // shards_of).reshape((-1,) + (1,) * (len(shape) - position - 1))

    gain = one(*split[0])
    for cut in split[1:]:
        gain = gain * one(*cut)
    return gain


def scatter_about(rng, dims, deviation, limit, split=(), held_as=jnp.bfloat16):
    level = steps_of(rng, dims, split, -0.22, 0.18) if split else 1.0
    drawn = jax.random.normal(rng, dims, jnp.float32) * deviation * level
    return jnp.minimum(jnp.maximum(drawn, -limit), limit).astype(held_as)


def setup_inputs(seed: int = 0) -> dict:
    splits = jax.random.split(jax.random.key(seed), 6)
    return {
        "preds": scatter_about(splits[0], (M, C, CELLS), 1.0, 6.0, ((0, 16), (2, 32))),
        "target": scatter_about(splits[1], (C, CELLS), 1.0, 6.0, ((1, 32),)),
        "area": jnp.clip(jnp.exp(math.log(1.0) - 2.3025851 * jax.random.uniform(splits[2], (CELLS,), jnp.float32) ** steps_of(splits[2], (CELLS,), ((0, 32),), -0.2, 0.2)), 0.1, 1.0),
        "channel_weight": jnp.clip(jnp.exp(jax.random.uniform(splits[3], (C,), jnp.float32, math.log(0.1), math.log(1.0))), 0.1, 1.0),
        "neighbours": draw_neighbours(jax.random.fold_in(splits[5], 71), 0),
    }


ALPHA = 0.5
DELTA = 0.1

def smooth(field, neighbours):
    total = jnp.zeros_like(field)
    for k in range(NEIGH):
        total = total + jnp.take(field, neighbours[k], axis=field.ndim - 1)
    return (1.0 - ALPHA) * field + ALPHA / NEIGH * total

def smooth_back(slope, neighbours):
    total = jnp.zeros_like(slope)
    for k in range(NEIGH):
        total = total.at[..., neighbours[k]].add(slope)
    return (1.0 - ALPHA) * slope + ALPHA / NEIGH * total

def crps_terms(members, truth, coef):
    count = members.shape[0]

    def step(carry, other):
        value, slope = carry
        diff = members - other[None]
        root = jnp.sqrt(diff * diff + DELTA * DELTA)
        return ((value + root - DELTA, slope + diff / root), None)
    zeros = jnp.zeros(members.shape, jnp.float32)
    (value, slope), _ = lax.scan(step, (zeros, zeros), members)
    direct = members - truth[None]
    root = jnp.sqrt(direct * direct + DELTA * DELTA)
    term = (root - DELTA) / count - value / (2.0 * count * (count - 1))
    loss = jnp.sum(coef[None] * term)
    gradient = coef[None] * (direct / root / count - slope / (count * (count - 1)))
    return (loss, gradient)

def reference(preds, target, area, channel_weight, neighbours):
    joined = jnp.concatenate([preds.astype(jnp.float32), target.astype(jnp.float32)[None]], axis=0)
    level_one = smooth(joined, neighbours)
    level_two = smooth(level_one, neighbours)
    level_four = smooth(smooth(level_two, neighbours), neighbours)
    coef = channel_weight[:, None] * area[None, :] / (jnp.sum(channel_weight) * jnp.sum(area))
    losses = []
    slopes = []
    for level in (joined, level_one, level_two, level_four):
        loss, gradient = crps_terms(level[:M], level[M], coef)
        losses.append(loss)
        slopes.append(gradient)
    grad = slopes[0] + smooth_back(slopes[1], neighbours)
    grad = grad + smooth_back(smooth_back(slopes[2], neighbours), neighbours)
    deep = slopes[3]
    for k in range(4):
        deep = smooth_back(deep, neighbours)
    grad = grad + deep
    return (jnp.stack(losses), grad)
```

```python
import functools

import jax
import jax.numpy as jnp
from jax import lax
from jax.experimental import pallas as pl
from jax.experimental.pallas import tpu as pltpu
from jax.sharding import PartitionSpec as P

GROUP = 4
CH = 2
M = 16
LANE = 128
NEIGH = 4
ROW = 720
BLOCK = 1024
PER = BLOCK // LANE
WIDTH = GROUP * BLOCK
CHUNKS = WIDTH // LANE
TILE = 256
REACH = 3
BAND = (2 * REACH + 1) * TILE
SIDE = 4 * REACH
OWN = WIDTH // TILE
EXT = (OWN + 2 * SIDE) * TILE
BLOCKS = OWN + 2 * SIDE - 2 * REACH
EDGE = 2 * SIDE - 1
RF = 40
HIGH = 48
RB = CH * M
RT = RB + CH
WIRE = -(-(EDGE * RT + RF - RT) // 8) * 8
AUX = (CH + NEIGH + 1) * PER
AREA_AT = (CH + NEIGH) * PER
NOTE = CH * PER + 1
DELTA = 0.1
F32 = jnp.float32
BF16 = jnp.bfloat16
SMEM_SPEC = pl.BlockSpec(memory_space=pltpu.SMEM)
VMEM_SPEC = pl.BlockSpec(memory_space=pltpu.VMEM)


def shape(*dims, dtype=F32):
    return jax.ShapeDtypeStruct(dims, dtype)


def call(body, name, outs, scratch=(), scalars=0, vectors=1, limit=24):
    return pl.pallas_call(
        body,
        in_specs=[SMEM_SPEC] * scalars + [VMEM_SPEC] * vectors,
        out_specs=[VMEM_SPEC] * len(outs),
        out_shape=outs,
        scratch_shapes=list(scratch),
        compiler_params=pltpu.CompilerParams(vmem_limit_bytes=limit * 1024 * 1024),
        name=name,
    )


def pack_body(preds_ref, send_ref):
    used = preds_ref.shape[1] // CH
    size = CH * PER
    send_ref[used * size :, :] = jnp.zeros((send_ref.shape[0] - used * size, LANE), F32)
    for c in range(CH):
        for l in range(PER):
            part = preds_ref[0, c * used : (c + 1) * used, l * LANE : (l + 1) * LANE].astype(F32)
            send_ref[pl.ds(c * PER + l, used, stride=size), :] = part


def shift_of(x, mine):
    return (mine - x + GROUP) % GROUP


def unpack_body(place_ref, recv_ref, side_ref, own_ref, left_ref, right_ref, rows, tight):
    rows[...] = jnp.zeros_like(rows)
    tight[...] = jnp.zeros_like(tight)
    for x in range(GROUP):
        for r in range(RT):
            if r < RB:
                c, m = divmod(r, M)
                value = recv_ref[m * GROUP + x, c * PER : (c + 1) * PER, :]
            else:
                c = r - RB
                value = side_ref[shift_of(x, place_ref[1]), c * PER : (c + 1) * PER, :]
            rows[pl.ds(x * PER * RF + r, PER, stride=RF), :] = value
            tight[pl.ds(x * PER * RT + r, PER, stride=RT), :] = value
    for i in range(CHUNKS):
        own_ref[i] = rows[i * RF : (i + 1) * RF, :]
    left_ref[...] = tight[:WIRE, :]
    start = (CHUNKS - EDGE) * RT
    right_ref[...] = tight[start : start + WIRE, :]


def parts(value):
    high = value.astype(BF16).astype(F32)
    return jnp.concatenate([high, value - high], axis=0).astype(BF16)


def tile_at(index, count=1):
    return pl.ds(pl.multiple_of(index * TILE, TILE), count * TILE)


def builder(row_group, mine, aux_ref, band, cells):
    down = lax.broadcasted_iota(jnp.int32, (TILE, TILE), 0)
    across = lax.broadcasted_iota(jnp.int32, (TILE, TILE), 1)
    unit = jnp.where(down == across, 0.5, 0.0).astype(BF16)
    count = down.astype(F32).astype(BF16)
    weight = jnp.full((TILE, TILE), 0.5 / NEIGH, BF16)
    none = jnp.zeros((TILE, TILE), BF16)
    first_cell = row_group * WIDTH - SIDE * TILE

    def hits(relative, t):
        at = relative - float(t * TILE)
        at = jnp.where((at < 0.0) | (at > TILE - 1.0), -1.0, at).astype(BF16)
        return jnp.where(count == at, weight, none)

    def places(b, k):
        halves = []
        for h in range(2):
            chunk = CHUNKS - 2 * SIDE + 2 * (b + REACH) + h
            x = (chunk % CHUNKS) // PER
            piece = (chunk // CHUNKS) * GROUP + shift_of(x, mine)
            halves.append(aux_ref[piece, pl.ds((CH + k) * PER + chunk % PER, 1), :])
        return jnp.concatenate(halves, axis=1) - (first_cell + b * TILE).astype(F32)

    def plain(b, h, stage):
        relative = [places(b, k) for k in range(NEIGH)]
        for t in range(2 * REACH + 1):
            total = hits(relative[2], t) + hits(relative[3], t)
            if t < 2:
                total = total + hits(relative[0], t)
            if t > 2 * REACH - 2:
                total = total + hits(relative[1], t)
            if t == REACH:
                total = total + unit
            span = slice(t * TILE, (t + 1) * TILE)
            stage[h, span, :] = total
            band[b, span, :] = total

    def clipped(b, h, stage):
        cell = first_cell + (b + REACH) * TILE

        def more(k, tiles):
            relative = places(b, k)
            for t in tiles:
                span = slice(t * TILE, (t + 1) * TILE)
                total = band[b, span, :] + hits(relative, t)
                stage[h, span, :] = total
                band[b, span, :] = total

        @pl.when(cell < ROW)
        def _():
            more(0, range(2, 2 * REACH + 1))

        @pl.when(cell + TILE > cells - ROW)
        def _():
            more(1, range(2 * REACH - 1))

    return plain, clipped


def scorer(weight_ref, mine, aux_ref, rows, slopes, sums):
    square = DELTA * DELTA
    sums[...] = jnp.zeros_like(sums)

    def one(level, index):
        c = index // GROUP
        x = index % GROUP
        base = level * (2 * BLOCKS * RF) + (2 * (SIDE - REACH) + x * PER) * RF
        fields = [rows[pl.ds(base + c * M + m, PER, stride=RF), :] for m in range(M)]
        truth = rows[pl.ds(base + RB + c, PER, stride=RF), :]
        coef = aux_ref[GROUP + shift_of(x, mine), AREA_AT:, :] * weight_ref[c]
        slope = [None] * M
        inverse = jnp.zeros((PER, LANE), F32)
        for a in range(M):
            for b in range(a + 1, M):
                diff = fields[a] - fields[b]
                r = lax.rsqrt(diff * diff + square)
                s = diff * r
                inverse = inverse + r
                slope[a] = s if slope[a] is None else slope[a] + s
                slope[b] = -s if slope[b] is None else slope[b] - s
        pair = square * inverse
        direct_sum = jnp.zeros((PER, LANE), F32)
        out = (level * CHUNKS + x * PER) * RB + c * M
        for m in range(M):
            direct = fields[m] - truth
            q = direct * direct + square
            r = lax.rsqrt(q)
            direct_sum = direct_sum + q * r
            pair = pair + direct * slope[m]
            slopes[pl.ds(out + m, PER, stride=RB), :] = coef * (
                direct * r * (1.0 / M) - slope[m] * (1.0 / (M * (M - 1)))
            )
        term = direct_sum * (1.0 / M) - pair * (1.0 / (M * (M - 1))) - 0.5 * DELTA
        span = slice(level * PER, (level + 1) * PER)
        sums[span, :] = sums[span, :] + coef * term

    return one


def main_body(
    cells, place_ref, weight_ref, own_ref, left_ref, right_ref, aux_ref,
    center_ref, outl_ref, outr_ref, loss_ref, band, xs, rows, slopes, total, sums, stage_a, stage_b,
):
    row_group = place_ref[0]
    mine = place_ref[1]
    plain, clipped = builder(row_group, mine, aux_ref, band, cells)
    score = scorer(weight_ref, mine, aux_ref, rows, slopes, sums)

    xs[0, :, :LANE] = jnp.zeros((2 * RF, LANE), BF16)
    xs[0, :, EXT - LANE :] = jnp.zeros((2 * RF, LANE), BF16)
    for i in range(EDGE):
        near = slice(i * RT, i * RT + RF)
        xs[0, :, (1 + i) * LANE : (2 + i) * LANE] = parts(left_ref[near, :])
        far = 2 * (SIDE + OWN) + i
        xs[0, :, far * LANE : (far + 1) * LANE] = parts(right_ref[near, :])
    for i in range(CHUNKS):
        value = own_ref[i]
        at = 2 * SIDE + i
        xs[0, :, at * LANE : (at + 1) * LANE] = parts(value)
        at = 2 * (SIDE - REACH) + i
        rows[at * RF : (at + 1) * RF, :] = value

    def products(step, p, read):
        got = []
        for h in range(2):
            b = 2 * p + h + step * REACH
            used = HIGH if step == 0 else 2 * RF
            field = xs[step % 2, :used, tile_at(b, 2 * REACH + 1)]
            got.append(jnp.dot(field, read(b, h), preferred_element_type=F32))
        return got

    def keep(step, p, got):
        kept = {0: 1, 1: 2, 3: 3}.get(step)
        for h in range(2):
            b = 2 * p + h + step * REACH
            value = got[h][:RF]
            if step > 0:
                value = value + got[h][RF:]
            if step < 3:
                xs[(step + 1) % 2, :, tile_at(b + REACH)] = parts(value)
            if kept is not None:
                start = pl.multiple_of(kept * (2 * BLOCKS * RF) + b * (2 * RF), RF)
                rows[pl.ds(start, RF), :] = value[:, :LANE]
                rows[pl.ds(start + RF, RF), :] = value[:, LANE:]

    def build_pair(p, stage):
        for h in range(2):
            plain(2 * p + h, h, stage)

    def fix_pair(p, stage):
        for h in range(2):
            clipped(2 * p + h, h, stage)

    def use_and_build(p, stage, following):
        got = products(0, p, lambda b, h: stage[h])
        build_pair(p + 1, following)
        keep(0, p, got)
        fix_pair(p + 1, following)

    build_pair(0, stage_a)
    fix_pair(0, stage_a)

    def two_pairs(i, carry):
        use_and_build(2 * i, stage_a, stage_b)
        use_and_build(2 * i + 1, stage_b, stage_a)
        return carry

    last = BLOCKS // 2 - 1
    lax.fori_loop(0, last // 2, two_pairs, 0)
    keep(0, last, products(0, last, lambda b, h: stage_a[h]))

    for step in range(1, 4):

        def forward(scored, p, carry):
            got = products(step, p, lambda b, h: band[b])
            if scored:
                score(step - 1, p)
            keep(step, p, got)
            return carry

        split = CH * GROUP
        lax.fori_loop(0, split, functools.partial(forward, True), 0)
        lax.fori_loop(split, BLOCKS // 2 - REACH * step, functools.partial(forward, False), 0)

    def only_score(index, carry):
        score(3, index)
        return carry

    lax.fori_loop(0, CH * GROUP, only_score, 0)
    partial = [jnp.sum(sums[level * PER : (level + 1) * PER, :], axis=0, keepdims=True) for level in range(4)]
    partial.append(jnp.sum(aux_ref[GROUP, AREA_AT:, :], axis=0, keepdims=True) * (1.0 / M))
    partial.append(jnp.zeros((PER - len(partial), LANE), F32))
    partial = jnp.concatenate(partial, axis=0)
    for i in range(loss_ref.shape[0]):
        loss_ref[i] = partial

    gs = xs.at[0]
    for step in range(4):
        first = (3 - step) * REACH
        level = {0: 3, 2: 2, 3: 1}.get(step)
        if step > 0 and level is not None:
            for i in range(CHUNKS):
                at = slice((2 * SIDE + i) * LANE, (2 * SIDE + i + 1) * LANE)
                begin = (level * CHUNKS + i) * RB
                total[:, at] = total[:, at] + slopes[begin : begin + RB, :]
        if step == 0:
            for i in range(CHUNKS):
                at = slice((2 * SIDE + i) * LANE, (2 * SIDE + i + 1) * LANE)
                begin = (level * CHUNKS + i) * RB
                gs[: 2 * RB, at] = parts(slopes[begin : begin + RB, :])
        else:

            def refill(p, carry):
                at = tile_at(p + first + REACH)
                gs[: 2 * RB, at] = parts(total[:, at])
                return carry

            lax.fori_loop(0, BLOCKS - 2 * first, refill, 0)
        total[...] = jnp.zeros_like(total)

        def backward(p, carry):
            got = []
            for h in range(2):
                b = 2 * p + h + first
                got.append(
                    lax.dot_general(
                        gs[: 2 * RB, tile_at(b + REACH)],
                        band[b],
                        (((1,), (1,)), ((), ())),
                        preferred_element_type=F32,
                    )
                )
            for h in range(2):
                at = tile_at(2 * p + h + first, 2 * REACH + 1)
                total[:, at] = total[:, at] + (got[h][:RB] + got[h][RB:])
            return carry

        lax.fori_loop(0, (BLOCKS - 2 * first) // 2, backward, 0)

    for i in range(CHUNKS):
        at = 2 * SIDE + i
        center_ref[i] = total[:, at * LANE : (at + 1) * LANE] + slopes[i * RB : (i + 1) * RB, :]
    for i in range(EDGE):
        outl_ref[i] = total[:, (1 + i) * LANE : (2 + i) * LANE]
        far = 2 * (SIDE + OWN) + i
        outr_ref[i] = total[:, far * LANE : (far + 1) * LANE]


def final_body(center_ref, arrl_ref, arrr_ref, sums_ref, send_ref, rows):
    for i in range(CHUNKS):
        value = center_ref[i]
        if i < EDGE:
            value = value + arrl_ref[i]
        if i >= CHUNKS - EDGE:
            value = value + arrr_ref[i - (CHUNKS - EDGE)]
        rows[i * RB : (i + 1) * RB, :] = value
    for x in range(GROUP):
        for c in range(CH):
            for m in range(M):
                start = (m * GROUP + x) * NOTE + c * PER
                send_ref[start : start + PER, :] = rows[pl.ds(x * PER * RB + c * M + m, PER, stride=RB), :]
    sums = sums_ref[0]
    for i in range(1, sums_ref.shape[0]):
        sums = sums + sums_ref[i]
    sums = jnp.sum(sums, axis=1, keepdims=True)
    down = lax.broadcasted_iota(jnp.int32, (PER, LANE), 0)
    across = lax.broadcasted_iota(jnp.int32, (PER, LANE), 1)
    note = jnp.sum(jnp.where(down == across, sums, 0.0), axis=0, keepdims=True)
    slots = send_ref.shape[0] // NOTE
    send_ref[pl.ds(NOTE - 1, slots, stride=NOTE), :] = jnp.broadcast_to(note, (slots, LANE))


def spread_body(recv_ref, weight_ref, losses_ref, out_ref):
    slots = recv_ref.shape[0] // NOTE
    sums = jnp.sum(recv_ref[pl.ds(NOTE - 1, slots, stride=NOTE), :], axis=0, keepdims=True)
    lane = lax.broadcasted_iota(jnp.int32, (1, LANE), 1)
    area = jnp.sum(jnp.where(lane == 4, sums, 0.0), axis=1, keepdims=True)
    scale = 1.0 / (jnp.sum(weight_ref[...], axis=1, keepdims=True) * area)
    losses_ref[...] = jnp.broadcast_to(sums * scale, losses_ref.shape)
    used = out_ref.shape[1] // CH
    for c in range(CH):
        for l in range(PER):
            part = recv_ref[pl.ds(c * PER + l, used, stride=NOTE), :]
            out_ref[0, c * used : (c + 1) * used, l * LANE : (l + 1) * LANE] = part * scale


def local(preds, target, area, channel_weight, neighbours):
    members = lax.axis_size("member")
    cells = lax.axis_size("cell")
    channels = preds.shape[1]
    member = lax.axis_index("member")
    cell = lax.axis_index("cell")
    slots = members * GROUP
    used = channels // CH
    rows = range(cells // GROUP)

    by_row = [[m * cells + y * GROUP + x for m in range(members) for x in range(GROUP)] for y in rows]

    def among_rows(move):
        return [(y * GROUP + x, move(y) * GROUP + x) for y in rows if move(y) in rows for x in range(GROUP)]

    def among_four(move):
        return [(y * GROUP + x, y * GROUP + move(x)) for y in rows for x in range(GROUP)]

    def exchange(to_left, to_right):
        return (
            lax.ppermute(to_right, "cell", among_rows(lambda y: y + 1)),
            lax.ppermute(to_left, "cell", among_rows(lambda y: y - 1)),
        )

    place = jnp.stack([cell // GROUP, cell % GROUP]).astype(jnp.int32)
    (send,) = call(pack_body, "pack", [shape(slots * CH * PER, LANE)])(preds)
    send, target, neighbours, area = lax.optimization_barrier((send, target, neighbours, area))
    recv = lax.all_to_all(
        send.reshape(slots, CH * PER, LANE), ("member", "cell"), 0, 0, axis_index_groups=by_row, tiled=True
    )

    by_slot = jnp.pad(target.astype(F32).reshape(CH, used, BLOCK), ((0, 0), (0, slots - used), (0, 0)))
    some = lax.dynamic_slice_in_dim(by_slot, member * GROUP, GROUP, 1)
    some = jnp.moveaxis(some, 1, 0).reshape(GROUP, CH * PER, LANE)
    common = jnp.concatenate([neighbours.astype(F32).reshape(NEIGH * PER, LANE), area.reshape(PER, LANE)])
    side = []
    for shift in range(GROUP):
        to = (cell + shift) % GROUP
        piece = jnp.concatenate([lax.dynamic_index_in_dim(some, to, 0, keepdims=False), common])
        if shift:
            piece = lax.ppermute(piece, "cell", among_four(lambda x: (x + shift) % GROUP))
        side.append(piece)
    side = jnp.stack(side)
    before, after = exchange(side, side)
    aux = jnp.concatenate([before, side, after])

    slot = member * GROUP + cell % GROUP
    weights = jnp.pad(channel_weight.reshape(CH, used), ((0, 0), (0, slots - used)))
    weights = lax.dynamic_index_in_dim(weights, slot, 1, keepdims=False)

    own, to_left, to_right = call(
        unpack_body,
        "unpack",
        [shape(CHUNKS, RF, LANE), shape(WIRE, LANE), shape(WIRE, LANE)],
        [pltpu.VMEM((CHUNKS * RF, LANE), F32), pltpu.VMEM((CHUNKS * RT + 16, LANE), F32)],
        scalars=1,
        vectors=2,
    )(place, recv, side)
    left, right = exchange(to_left, to_right)

    center, out_left, out_right, sums = call(
        functools.partial(main_body, cells * BLOCK),
        "smooth_score_back",
        [shape(CHUNKS, RB, LANE), shape(EDGE, RB, LANE), shape(EDGE, RB, LANE), shape(len(rows), PER, LANE)],
        [
            pltpu.VMEM((BLOCKS, BAND, TILE), BF16),
            pltpu.VMEM((2, 2 * RF, EXT), BF16),
            pltpu.VMEM((4 * 2 * BLOCKS * RF, LANE), F32),
            pltpu.VMEM((4 * CHUNKS * RB, LANE), F32),
            pltpu.VMEM((RB, EXT), F32),
            pltpu.VMEM((4 * PER, LANE), F32),
            pltpu.VMEM((2, BAND, TILE), BF16),
            pltpu.VMEM((2, BAND, TILE), BF16),
        ],
        scalars=2,
        vectors=4,
        limit=58,
    )(place, weights, own, left, right, aux)

    arrived = exchange(out_left, out_right)
    by_column = [[y * GROUP + x for y in rows] for x in range(GROUP)]
    sums = lax.all_to_all(sums, "cell", 0, 0, axis_index_groups=by_column, tiled=True)

    (packed,) = call(
        final_body,
        "gather_grad",
        [shape(slots * NOTE, LANE)],
        [pltpu.VMEM((CHUNKS * RB, LANE), F32)],
        vectors=4,
    )(center, *arrived, sums)
    back = lax.all_to_all(
        packed.reshape(slots, 1, NOTE * LANE), ("member", "cell"), 0, 0, axis_index_groups=by_row, tiled=True
    )
    losses, grad = call(spread_body, "spread", [shape(PER, LANE), shape(1, channels, BLOCK)], vectors=2)(
        back.reshape(slots * NOTE, LANE), jnp.pad(channel_weight, (0, LANE - channels)).reshape(1, LANE)
    )
    return losses[0, :4], grad


def solution(mesh):
    in_specs = (P("member", None, "cell"), P(None, "cell"), P("cell"), P(), P(None, "cell"))
    out_specs = (P(), P("member", None, "cell"))
    return jax.shard_map(local, mesh=mesh, in_specs=in_specs, out_specs=out_specs, check_vma=False)
```

```python
import functools

import jax
import jax.numpy as jnp
from jax import lax
from jax.experimental import pallas as pl
from jax.experimental.pallas import tpu as pltpu
from jax.sharding import PartitionSpec as P

GROUP = 4
CH = 2
M = 16
LANE = 128
NEIGH = 4
ROW = 720
BLOCK = 1024
PER = BLOCK // LANE
WIDTH = GROUP * BLOCK
CHUNKS = WIDTH // LANE
TILE = 256
REACH = 3
BAND = (2 * REACH + 1) * TILE
SIDE = 4 * REACH
OWN = WIDTH // TILE
EXT = (OWN + 2 * SIDE) * TILE
BLOCKS = OWN + 2 * SIDE - 2 * REACH
EDGE = 2 * SIDE - 1
RF = 40
HIGH = 48
RB = CH * M
RT = RB + CH
WIRE = -(-(EDGE * RT + RF - RT) // 8) * 8
AUX = (CH + NEIGH + 1) * PER
AREA_AT = (CH + NEIGH) * PER
NOTE = CH * PER + 1
DELTA = 0.1
F32 = jnp.float32
BF16 = jnp.bfloat16
SMEM_SPEC = pl.BlockSpec(memory_space=pltpu.SMEM)
VMEM_SPEC = pl.BlockSpec(memory_space=pltpu.VMEM)


def shape(*dims, dtype=F32):
    return jax.ShapeDtypeStruct(dims, dtype)


def call(body, name, outs, scratch=(), scalars=0, vectors=1, limit=24):
    return pl.pallas_call(
        body,
        in_specs=[SMEM_SPEC] * scalars + [VMEM_SPEC] * vectors,
        out_specs=[VMEM_SPEC] * len(outs),
        out_shape=outs,
        scratch_shapes=list(scratch),
        compiler_params=pltpu.CompilerParams(vmem_limit_bytes=limit * 1024 * 1024),
        name=name,
    )


def pack_body(preds_ref, send_ref):
    used = preds_ref.shape[1] // CH
    size = CH * PER
    send_ref[used * size :, :] = jnp.zeros((send_ref.shape[0] - used * size, LANE), F32)
    for c in range(CH):
        for l in range(PER):
            part = preds_ref[0, c * used : (c + 1) * used, l * LANE : (l + 1) * LANE].astype(F32)
            send_ref[pl.ds(c * PER + l, used, stride=size), :] = part


def shift_of(x, mine):
    return (mine - x + GROUP) % GROUP


def unpack_body(place_ref, recv_ref, side_ref, own_ref, left_ref, right_ref, rows, tight):
    rows[...] = jnp.zeros_like(rows)
    tight[...] = jnp.zeros_like(tight)
    for x in range(GROUP):
        for r in range(RT):
            if r < RB:
                c, m = divmod(r, M)
                value = recv_ref[m * GROUP + x, c * PER : (c + 1) * PER, :]
            else:
                c = r - RB
                value = side_ref[shift_of(x, place_ref[1]), c * PER : (c + 1) * PER, :]
            rows[pl.ds(x * PER * RF + r, PER, stride=RF), :] = value
            tight[pl.ds(x * PER * RT + r, PER, stride=RT), :] = value
    for i in range(CHUNKS):
        own_ref[i] = rows[i * RF : (i + 1) * RF, :]
    left_ref[...] = tight[:WIRE, :]
    start = (CHUNKS - EDGE) * RT
    right_ref[...] = tight[start : start + WIRE, :]


def parts(value):
    high = value.astype(BF16).astype(F32)
    return jnp.concatenate([high, value - high], axis=0).astype(BF16)


def tile_at(index, count=1):
    return pl.ds(pl.multiple_of(index * TILE, TILE), count * TILE)


def builder(row_group, mine, aux_ref, band, pattern, cells):
    down = lax.broadcasted_iota(jnp.int32, (TILE, TILE), 0).astype(F32)
    across = lax.broadcasted_iota(jnp.int32, (1, TILE), 1).astype(F32)
    share = 0.5 / NEIGH
    first_cell = row_group * WIDTH - SIDE * TILE
    own = REACH * TILE
    fixed = (own - ROW, own + ROW)

    def hits(place, t):
        return jnp.where(down == place - float(t * TILE), share, 0.0)

    for t in range(2 * REACH + 1):
        total = hits(across + float(fixed[0]), t) + hits(across + float(fixed[1]), t)
        if t == REACH:
            total = total + NEIGH * hits(across + float(own), t)
        pattern[t * TILE : (t + 1) * TILE, :] = total.astype(BF16)

    def places(b, k):
        halves = []
        for h in range(2):
            chunk = CHUNKS - 2 * SIDE + 2 * (b + REACH) + h
            x = (chunk % CHUNKS) // PER
            piece = (chunk // CHUNKS) * GROUP + shift_of(x, mine)
            halves.append(aux_ref[piece, pl.ds((CH + k) * PER + chunk % PER, 1), :])
        return jnp.concatenate(halves, axis=1) - (first_cell + b * TILE).astype(F32)

    def plain(b, h, stage):
        near, far = [], []
        for k in (2, 3):
            place = places(b, k)
            high = jnp.floor(place * (1.0 / LANE))
            near.append(jnp.where(down[:LANE] == place - high * LANE, share, 0.0).astype(BF16))
            far.append(high)
        for t in range(BAND // LANE):
            span = slice(t * LANE, (t + 1) * LANE)
            total = pattern[span, :]
            for k in range(2):
                total = total + near[k] * jnp.where(far[k] == float(t), 1.0, 0.0).astype(BF16)
            stage[h, span, :] = total
            band[b, span, :] = total

    def clipped(b, h, stage):
        cell = first_cell + (b + REACH) * TILE

        def correct(k):
            place = places(b, k)
            for t in range(2 * REACH + 1):
                span = slice(t * TILE, (t + 1) * TILE)
                change = hits(place, t) - hits(across + float(fixed[k]), t)
                total = band[b, span, :] + change.astype(BF16)
                stage[h, span, :] = total
                band[b, span, :] = total

        @pl.when((cell >= 0) & (cell < ROW))
        def _():
            correct(0)

        @pl.when((cell < cells) & (cell + TILE > cells - ROW))
        def _():
            correct(1)

    return plain, clipped


def scorer(weight_ref, mine, aux_ref, rows, slopes, sums):
    square = DELTA * DELTA
    sums[...] = jnp.zeros_like(sums)

    def one(level, index):
        c = index // GROUP
        x = index % GROUP
        base = level * (2 * BLOCKS * RF) + (2 * (SIDE - REACH) + x * PER) * RF
        fields = [rows[pl.ds(base + c * M + m, PER, stride=RF), :] for m in range(M)]
        truth = rows[pl.ds(base + RB + c, PER, stride=RF), :]
        coef = aux_ref[GROUP + shift_of(x, mine), AREA_AT:, :] * weight_ref[c]
        slope = [None] * M
        inverse = jnp.zeros((PER, LANE), F32)
        for a in range(M):
            for b in range(a + 1, M):
                diff = fields[a] - fields[b]
                r = lax.rsqrt(diff * diff + square)
                s = diff * r
                inverse = inverse + r
                slope[a] = s if slope[a] is None else slope[a] + s
                slope[b] = -s if slope[b] is None else slope[b] - s
        pair = square * inverse
        direct_sum = jnp.zeros((PER, LANE), F32)
        out = (level * CHUNKS + x * PER) * RB + c * M
        for m in range(M):
            direct = fields[m] - truth
            q = direct * direct + square
            r = lax.rsqrt(q)
            direct_sum = direct_sum + q * r
            pair = pair + direct * slope[m]
            slopes[pl.ds(out + m, PER, stride=RB), :] = coef * (
                direct * r * (1.0 / M) - slope[m] * (1.0 / (M * (M - 1)))
            )
        term = direct_sum * (1.0 / M) - pair * (1.0 / (M * (M - 1))) - 0.5 * DELTA
        span = slice(level * PER, (level + 1) * PER)
        sums[span, :] = sums[span, :] + coef * term

    return one


def main_body(
    cells, place_ref, weight_ref, own_ref, left_ref, right_ref, aux_ref,
    center_ref, outl_ref, outr_ref, loss_ref, band, xs, rows, slopes, total, sums, stage_a, stage_b, pattern,
):
    row_group = place_ref[0]
    mine = place_ref[1]
    plain, clipped = builder(row_group, mine, aux_ref, band, pattern, cells)
    score = scorer(weight_ref, mine, aux_ref, rows, slopes, sums)

    xs[0, :, :LANE] = jnp.zeros((2 * RF, LANE), BF16)
    xs[0, :, EXT - LANE :] = jnp.zeros((2 * RF, LANE), BF16)
    for i in range(EDGE):
        near = slice(i * RT, i * RT + RF)
        xs[0, :, (1 + i) * LANE : (2 + i) * LANE] = parts(left_ref[near, :])
        far = 2 * (SIDE + OWN) + i
        xs[0, :, far * LANE : (far + 1) * LANE] = parts(right_ref[near, :])
    for i in range(CHUNKS):
        value = own_ref[i]
        at = 2 * SIDE + i
        xs[0, :, at * LANE : (at + 1) * LANE] = parts(value)
        at = 2 * (SIDE - REACH) + i
        rows[at * RF : (at + 1) * RF, :] = value

    def products(step, p, read):
        got = []
        for h in range(2):
            b = 2 * p + h + step * REACH
            used = HIGH if step == 0 else 2 * RF
            field = xs[step % 2, :used, tile_at(b, 2 * REACH + 1)]
            got.append(jnp.dot(field, read(b, h), preferred_element_type=F32))
        return got

    def keep(step, p, got):
        kept = {0: 1, 1: 2, 3: 3}.get(step)
        for h in range(2):
            b = 2 * p + h + step * REACH
            value = got[h][:RF]
            if step > 0:
                value = value + got[h][RF:]
            if step < 3:
                xs[(step + 1) % 2, :, tile_at(b + REACH)] = parts(value)
            if kept is not None:
                start = pl.multiple_of(kept * (2 * BLOCKS * RF) + b * (2 * RF), RF)
                rows[pl.ds(start, RF), :] = value[:, :LANE]
                rows[pl.ds(start + RF, RF), :] = value[:, LANE:]

    def build_pair(p, stage):
        for h in range(2):
            plain(2 * p + h, h, stage)

    def fix_pair(p, stage):
        for h in range(2):
            clipped(2 * p + h, h, stage)

    def use_and_build(p, stage, following):
        got = products(0, p, lambda b, h: stage[h])
        build_pair(p + 1, following)
        keep(0, p, got)
        fix_pair(p + 1, following)

    build_pair(0, stage_a)
    fix_pair(0, stage_a)

    def two_pairs(i, carry):
        use_and_build(2 * i, stage_a, stage_b)
        use_and_build(2 * i + 1, stage_b, stage_a)
        return carry

    last = BLOCKS // 2 - 1
    lax.fori_loop(0, last // 2, two_pairs, 0)
    keep(0, last, products(0, last, lambda b, h: stage_a[h]))

    for step in range(1, 4):

        def forward(scored, p, carry):
            got = products(step, p, lambda b, h: band[b])
            if scored:
                score(step - 1, p)
            keep(step, p, got)
            return carry

        split = CH * GROUP
        lax.fori_loop(0, split, functools.partial(forward, True), 0)
        lax.fori_loop(split, BLOCKS // 2 - REACH * step, functools.partial(forward, False), 0)

    def only_score(index, carry):
        score(3, index)
        return carry

    lax.fori_loop(0, CH * GROUP, only_score, 0)
    partial = [jnp.sum(sums[level * PER : (level + 1) * PER, :], axis=0, keepdims=True) for level in range(4)]
    partial.append(jnp.sum(aux_ref[GROUP, AREA_AT:, :], axis=0, keepdims=True) * (1.0 / M))
    partial.append(jnp.zeros((PER - len(partial), LANE), F32))
    partial = jnp.concatenate(partial, axis=0)
    for i in range(loss_ref.shape[0]):
        loss_ref[i] = partial

    gs = xs.at[0]
    for step in range(4):
        first = (3 - step) * REACH
        level = {0: 3, 2: 2, 3: 1}.get(step)
        if step > 0 and level is not None:
            for i in range(CHUNKS):
                at = slice((2 * SIDE + i) * LANE, (2 * SIDE + i + 1) * LANE)
                begin = (level * CHUNKS + i) * RB
                total[:, at] = total[:, at] + slopes[begin : begin + RB, :]
        if step == 0:
            for i in range(CHUNKS):
                at = slice((2 * SIDE + i) * LANE, (2 * SIDE + i + 1) * LANE)
                begin = (level * CHUNKS + i) * RB
                gs[: 2 * RB, at] = parts(slopes[begin : begin + RB, :])
        else:

            def refill(p, carry):
                at = tile_at(p + first + REACH)
                gs[: 2 * RB, at] = parts(total[:, at])
                return carry

            lax.fori_loop(0, BLOCKS - 2 * first, refill, 0)
        total[...] = jnp.zeros_like(total)

        def backward(p, carry):
            got = []
            for h in range(2):
                b = 2 * p + h + first
                got.append(
                    lax.dot_general(
                        gs[: 2 * RB, tile_at(b + REACH)],
                        band[b],
                        (((1,), (1,)), ((), ())),
                        preferred_element_type=F32,
                    )
                )
            one, two = (value[:RB] + value[RB:] for value in got)
            at = tile_at(2 * p + first)
            total[:, at] = total[:, at] + one[:, :TILE]
            at = tile_at(2 * p + first + 1, 2 * REACH)
            total[:, at] = total[:, at] + (one[:, TILE:] + two[:, :-TILE])
            at = tile_at(2 * p + first + 2 * REACH + 1)
            total[:, at] = total[:, at] + two[:, -TILE:]
            return carry

        lax.fori_loop(0, (BLOCKS - 2 * first) // 2, backward, 0)

    for i in range(CHUNKS):
        at = 2 * SIDE + i
        center_ref[i] = total[:, at * LANE : (at + 1) * LANE] + slopes[i * RB : (i + 1) * RB, :]
    for i in range(EDGE):
        outl_ref[i] = total[:, (1 + i) * LANE : (2 + i) * LANE]
        far = 2 * (SIDE + OWN) + i
        outr_ref[i] = total[:, far * LANE : (far + 1) * LANE]


def final_body(center_ref, arrl_ref, arrr_ref, sums_ref, send_ref, rows):
    for i in range(CHUNKS):
        value = center_ref[i]
        if i < EDGE:
            value = value + arrl_ref[i]
        if i >= CHUNKS - EDGE:
            value = value + arrr_ref[i - (CHUNKS - EDGE)]
        rows[i * RB : (i + 1) * RB, :] = value
    for x in range(GROUP):
        for c in range(CH):
            for m in range(M):
                start = (m * GROUP + x) * NOTE + c * PER
                send_ref[start : start + PER, :] = rows[pl.ds(x * PER * RB + c * M + m, PER, stride=RB), :]
    sums = sums_ref[0]
    for i in range(1, sums_ref.shape[0]):
        sums = sums + sums_ref[i]
    sums = jnp.sum(sums, axis=1, keepdims=True)
    down = lax.broadcasted_iota(jnp.int32, (PER, LANE), 0)
    across = lax.broadcasted_iota(jnp.int32, (PER, LANE), 1)
    note = jnp.sum(jnp.where(down == across, sums, 0.0), axis=0, keepdims=True)
    slots = send_ref.shape[0] // NOTE
    send_ref[pl.ds(NOTE - 1, slots, stride=NOTE), :] = jnp.broadcast_to(note, (slots, LANE))


def spread_body(recv_ref, weight_ref, losses_ref, out_ref):
    slots = recv_ref.shape[0] // NOTE
    sums = jnp.sum(recv_ref[pl.ds(NOTE - 1, slots, stride=NOTE), :], axis=0, keepdims=True)
    lane = lax.broadcasted_iota(jnp.int32, (1, LANE), 1)
    area = jnp.sum(jnp.where(lane == 4, sums, 0.0), axis=1, keepdims=True)
    scale = 1.0 / (jnp.sum(weight_ref[...], axis=1, keepdims=True) * area)
    losses = sums * scale
    for level in range(losses_ref.shape[0]):
        losses_ref[level] = losses[0, level]
    used = out_ref.shape[0] // (CH * PER)
    for c in range(CH):
        for q in range(used):
            part = recv_ref[q * NOTE + c * PER : q * NOTE + (c + 1) * PER, :]
            out_ref[(c * used + q) * PER : (c * used + q + 1) * PER, :] = part * scale


def local(preds, target, area, channel_weight, neighbours):
    members = lax.axis_size("member")
    cells = lax.axis_size("cell")
    channels = preds.shape[1]
    member = lax.axis_index("member")
    cell = lax.axis_index("cell")
    slots = members * GROUP
    used = channels // CH
    rows = range(cells // GROUP)

    by_row = [[m * cells + y * GROUP + x for m in range(members) for x in range(GROUP)] for y in rows]

    def among_rows(move):
        return [(y * GROUP + x, move(y) * GROUP + x) for y in rows if move(y) in rows for x in range(GROUP)]

    def among_four(move):
        return [(y * GROUP + x, y * GROUP + move(x)) for y in rows for x in range(GROUP)]

    def exchange(to_left, to_right):
        return (
            lax.ppermute(to_right, "cell", among_rows(lambda y: y + 1)),
            lax.ppermute(to_left, "cell", among_rows(lambda y: y - 1)),
        )

    place = jnp.stack([cell // GROUP, cell % GROUP]).astype(jnp.int32)
    (send,) = call(pack_body, "pack", [shape(slots * CH * PER, LANE)])(preds)
    send, target, neighbours, area = lax.optimization_barrier((send, target, neighbours, area))
    recv = lax.all_to_all(
        send.reshape(slots, CH * PER, LANE), ("member", "cell"), 0, 0, axis_index_groups=by_row, tiled=True
    )

    by_slot = jnp.pad(target.astype(F32).reshape(CH, used, BLOCK), ((0, 0), (0, slots - used), (0, 0)))
    some = lax.dynamic_slice_in_dim(by_slot, member * GROUP, GROUP, 1)
    some = jnp.moveaxis(some, 1, 0).reshape(GROUP, CH * PER, LANE)
    common = jnp.concatenate([neighbours.astype(F32).reshape(NEIGH * PER, LANE), area.reshape(PER, LANE)])
    side = []
    for shift in range(GROUP):
        to = (cell + shift) % GROUP
        piece = jnp.concatenate([lax.dynamic_index_in_dim(some, to, 0, keepdims=False), common])
        if shift:
            piece = lax.ppermute(piece, "cell", among_four(lambda x: (x + shift) % GROUP))
        side.append(piece)
    side = jnp.stack(side)
    slot = member * GROUP + cell % GROUP
    weights = jnp.pad(channel_weight.reshape(CH, used), ((0, 0), (0, slots - used)))
    weights = lax.dynamic_index_in_dim(weights, slot, 1, keepdims=False)

    own, to_left, to_right = call(
        unpack_body,
        "unpack",
        [shape(CHUNKS, RF, LANE), shape(WIRE, LANE), shape(WIRE, LANE)],
        [pltpu.VMEM((CHUNKS * RF, LANE), F32), pltpu.VMEM((CHUNKS * RT + 16, LANE), F32)],
        scalars=1,
        vectors=2,
    )(place, recv, side)
    own, side, to_left, to_right = lax.optimization_barrier((own, side, to_left, to_right))
    left, right = exchange(to_left, to_right)
    before, after = exchange(side, side)
    aux = jnp.concatenate([before, side, after])

    center, out_left, out_right, sums = call(
        functools.partial(main_body, cells * BLOCK),
        "smooth_score_back",
        [shape(CHUNKS, RB, LANE), shape(EDGE, RB, LANE), shape(EDGE, RB, LANE), shape(len(rows), PER, LANE)],
        [
            pltpu.VMEM((BLOCKS, BAND, TILE), BF16),
            pltpu.VMEM((2, 2 * RF, EXT), BF16),
            pltpu.VMEM((4 * 2 * BLOCKS * RF, LANE), F32),
            pltpu.VMEM((4 * CHUNKS * RB, LANE), F32),
            pltpu.VMEM((RB, EXT), F32),
            pltpu.VMEM((4 * PER, LANE), F32),
            pltpu.VMEM((2, BAND, TILE), BF16),
            pltpu.VMEM((2, BAND, TILE), BF16),
            pltpu.VMEM((BAND, TILE), BF16),
        ],
        scalars=2,
        vectors=4,
        limit=58,
    )(place, weights, own, left, right, aux)

    arrived = exchange(out_left, out_right)
    by_column = [[y * GROUP + x for y in rows] for x in range(GROUP)]
    sums = lax.all_to_all(sums, "cell", 0, 0, axis_index_groups=by_column, tiled=True)

    (packed,) = call(
        final_body,
        "gather_grad",
        [shape(slots * NOTE, LANE)],
        [pltpu.VMEM((CHUNKS * RB, LANE), F32)],
        vectors=4,
    )(center, *arrived, sums)
    back = lax.all_to_all(
        packed.reshape(slots, 1, NOTE * LANE), ("member", "cell"), 0, 0, axis_index_groups=by_row, tiled=True
    )
    losses, grad = pl.pallas_call(
        spread_body,
        in_specs=[VMEM_SPEC] * 2,
        out_specs=[SMEM_SPEC, VMEM_SPEC],
        out_shape=[shape(4), shape(channels * PER, LANE)],
        compiler_params=pltpu.CompilerParams(vmem_limit_bytes=24 * 1024 * 1024),
        name="spread",
    )(back.reshape(slots * NOTE, LANE), jnp.pad(channel_weight, (0, LANE - channels)).reshape(1, LANE))
    return losses, grad.reshape(1, channels, BLOCK)


def solution(mesh):
    in_specs = (P("member", None, "cell"), P(None, "cell"), P("cell"), P(), P(None, "cell"))
    out_specs = (P(), P("member", None, "cell"))
    return jax.shard_map(local, mesh=mesh, in_specs=in_specs, out_specs=out_specs, check_vma=False)
```

```python
import functools

import jax
import jax.numpy as jnp
from jax import lax
from jax.experimental import pallas as pl
from jax.experimental.pallas import tpu as pltpu
from jax.sharding import PartitionSpec as P

GROUP = 4
CH = 2
M = 16
LANE = 128
NEIGH = 4
ROW = 720
BLOCK = 1024
PER = BLOCK // LANE
WIDTH = GROUP * BLOCK
CHUNKS = WIDTH // LANE
TILE = 256
REACH = 3
BAND = (2 * REACH + 1) * TILE
SIDE = 4 * REACH
OWN = WIDTH // TILE
EXT = (OWN + 2 * SIDE) * TILE
BLOCKS = OWN + 2 * SIDE - 2 * REACH
EDGE = 2 * SIDE - 1
RUN = 4
RF = 40
HIGH = 48
RB = CH * M
RT = RB + CH
WIRE = -(-(EDGE * RT + RF - RT) // 8) * 8
AUX = (CH + NEIGH + 1) * PER
AREA_AT = (CH + NEIGH) * PER
NOTE = CH * PER + 1
DELTA = 0.1
F32 = jnp.float32
BF16 = jnp.bfloat16
SMEM_SPEC = pl.BlockSpec(memory_space=pltpu.SMEM)
VMEM_SPEC = pl.BlockSpec(memory_space=pltpu.VMEM)


def shape(*dims, dtype=F32):
    return jax.ShapeDtypeStruct(dims, dtype)


def call(body, name, outs, scratch=(), scalars=0, vectors=1, limit=24):
    return pl.pallas_call(
        body,
        in_specs=[SMEM_SPEC] * scalars + [VMEM_SPEC] * vectors,
        out_specs=[VMEM_SPEC] * len(outs),
        out_shape=outs,
        scratch_shapes=list(scratch),
        compiler_params=pltpu.CompilerParams(vmem_limit_bytes=limit * 1024 * 1024),
        name=name,
    )


def pack_body(preds_ref, send_ref):
    used = preds_ref.shape[1] // CH
    size = CH * PER
    send_ref[used * size :, :] = jnp.zeros((send_ref.shape[0] - used * size, LANE), F32)
    for c in range(CH):
        for l in range(PER):
            part = preds_ref[0, c * used : (c + 1) * used, l * LANE : (l + 1) * LANE].astype(F32)
            send_ref[pl.ds(c * PER + l, used, stride=size), :] = part


def shift_of(x, mine):
    return (mine - x + GROUP) % GROUP


def unpack_body(place_ref, recv_ref, side_ref, own_ref, left_ref, right_ref, rows, tight):
    rows[...] = jnp.zeros_like(rows)
    tight[...] = jnp.zeros_like(tight)
    for x in range(GROUP):
        for r in range(RT):
            if r < RB:
                c, m = divmod(r, M)
                value = recv_ref[m * GROUP + x, c * PER : (c + 1) * PER, :]
            else:
                c = r - RB
                value = side_ref[shift_of(x, place_ref[1]), c * PER : (c + 1) * PER, :]
            rows[pl.ds(x * PER * RF + r, PER, stride=RF), :] = value
            tight[pl.ds(x * PER * RT + r, PER, stride=RT), :] = value
    for i in range(CHUNKS):
        own_ref[i] = rows[i * RF : (i + 1) * RF, :]
    left_ref[...] = tight[:WIRE, :]
    start = (CHUNKS - EDGE) * RT
    right_ref[...] = tight[start : start + WIRE, :]


def parts(value):
    high = value.astype(BF16).astype(F32)
    return jnp.concatenate([high, value - high], axis=0).astype(BF16)


def tile_at(index, count=1):
    return pl.ds(pl.multiple_of(index * TILE, TILE), count * TILE)


def builder(row_group, mine, aux_ref, band, pattern, cells):
    down = lax.broadcasted_iota(jnp.int32, (TILE, TILE), 0).astype(F32)
    across = lax.broadcasted_iota(jnp.int32, (1, TILE), 1).astype(F32)
    share = 0.5 / NEIGH
    first_cell = row_group * WIDTH - SIDE * TILE
    own = REACH * TILE
    fixed = (own - ROW, own + ROW)

    def hits(place, t):
        return jnp.where(down == place - float(t * TILE), share, 0.0)

    for t in range(2 * REACH + 1):
        total = hits(across + float(fixed[0]), t) + hits(across + float(fixed[1]), t)
        if t == REACH:
            total = total + NEIGH * hits(across + float(own), t)
        pattern[t * TILE : (t + 1) * TILE, :] = total.astype(BF16)

    def places(b, k):
        halves = []
        for h in range(2):
            chunk = CHUNKS - 2 * SIDE + 2 * (b + REACH) + h
            x = (chunk % CHUNKS) // PER
            piece = (chunk // CHUNKS) * GROUP + shift_of(x, mine)
            halves.append(aux_ref[piece, pl.ds((CH + k) * PER + chunk % PER, 1), :])
        return jnp.concatenate(halves, axis=1) - (first_cell + b * TILE).astype(F32)

    def plain(b, h, stage):
        near, far = [], []
        for k in (2, 3):
            place = places(b, k)
            high = jnp.floor(place * (1.0 / LANE))
            near.append(jnp.where(down[:LANE] == place - high * LANE, share, 0.0).astype(BF16))
            far.append(high)
        for t in range(BAND // LANE):
            span = slice(t * LANE, (t + 1) * LANE)
            total = pattern[span, :]
            for k in range(2):
                total = total + near[k] * jnp.where(far[k] == float(t), 1.0, 0.0).astype(BF16)
            stage[h, span, :] = total
            band[b, span, :] = total

    def clipped(b, h, stage):
        cell = first_cell + (b + REACH) * TILE

        def correct(k):
            place = places(b, k)
            for t in range(2 * REACH + 1):
                span = slice(t * TILE, (t + 1) * TILE)
                change = hits(place, t) - hits(across + float(fixed[k]), t)
                total = band[b, span, :] + change.astype(BF16)
                stage[h, span, :] = total
                band[b, span, :] = total

        @pl.when((cell >= 0) & (cell < ROW))
        def _():
            correct(0)

        @pl.when((cell < cells) & (cell + TILE > cells - ROW))
        def _():
            correct(1)

    return plain, clipped


def scorer(weight_ref, mine, aux_ref, rows, slopes, sums):
    square = DELTA * DELTA
    sums[...] = jnp.zeros_like(sums)

    def one(level, index):
        c = index // GROUP
        x = index % GROUP
        base = level * (2 * BLOCKS * RF) + (2 * (SIDE - REACH) + x * PER) * RF
        fields = [rows[pl.ds(base + c * M + m, PER, stride=RF), :] for m in range(M)]
        truth = rows[pl.ds(base + RB + c, PER, stride=RF), :]
        coef = aux_ref[GROUP + shift_of(x, mine), AREA_AT:, :] * weight_ref[c]
        slope = [None] * M
        inverse = jnp.zeros((PER, LANE), F32)
        for a in range(M):
            for b in range(a + 1, M):
                diff = fields[a] - fields[b]
                r = lax.rsqrt(diff * diff + square)
                s = diff * r
                inverse = inverse + r
                slope[a] = s if slope[a] is None else slope[a] + s
                slope[b] = -s if slope[b] is None else slope[b] - s
        pair = square * inverse
        direct_sum = jnp.zeros((PER, LANE), F32)
        out = (level * CHUNKS + x * PER) * RB + c * M
        for m in range(M):
            direct = fields[m] - truth
            q = direct * direct + square
            r = lax.rsqrt(q)
            direct_sum = direct_sum + q * r
            pair = pair + direct * slope[m]
            slopes[pl.ds(out + m, PER, stride=RB), :] = coef * (
                direct * r * (1.0 / M) - slope[m] * (1.0 / (M * (M - 1)))
            )
        term = direct_sum * (1.0 / M) - pair * (1.0 / (M * (M - 1))) - 0.5 * DELTA
        span = slice(level * PER, (level + 1) * PER)
        sums[span, :] = sums[span, :] + coef * term

    return one


def main_body(
    cells, place_ref, weight_ref, own_ref, left_ref, right_ref, aux_ref,
    center_ref, outl_ref, outr_ref, loss_ref, band, xs, rows, slopes, total, sums, stage_a, stage_b, pattern,
):
    row_group = place_ref[0]
    mine = place_ref[1]
    plain, clipped = builder(row_group, mine, aux_ref, band, pattern, cells)
    score = scorer(weight_ref, mine, aux_ref, rows, slopes, sums)

    xs[0, :, :LANE] = jnp.zeros((2 * RF, LANE), BF16)
    xs[0, :, EXT - LANE :] = jnp.zeros((2 * RF, LANE), BF16)
    for i in range(EDGE):
        near = slice(i * RT, i * RT + RF)
        xs[0, :, (1 + i) * LANE : (2 + i) * LANE] = parts(left_ref[near, :])
        far = 2 * (SIDE + OWN) + i
        xs[0, :, far * LANE : (far + 1) * LANE] = parts(right_ref[near, :])
    for i in range(CHUNKS):
        value = own_ref[i]
        at = 2 * SIDE + i
        xs[0, :, at * LANE : (at + 1) * LANE] = parts(value)
        at = 2 * (SIDE - REACH) + i
        rows[at * RF : (at + 1) * RF, :] = value

    def products(step, begin, count, read):
        used = HIGH if step == 0 else 2 * RF
        got = []
        for h in range(count):
            b = begin + h + step * REACH
            field = xs[step % 2, :used, tile_at(b, 2 * REACH + 1)]
            got.append(jnp.dot(field, read(b, h), preferred_element_type=F32))
        return got

    def keep(step, begin, got):
        kept = {0: 1, 1: 2, 3: 3}.get(step)
        for h, value in enumerate(got):
            b = begin + h + step * REACH
            value = value[:RF] if step == 0 else value[:RF] + value[RF:]
            if step < 3:
                xs[(step + 1) % 2, :, tile_at(b + REACH)] = parts(value)
            if kept is not None:
                start = pl.multiple_of(kept * (2 * BLOCKS * RF) + b * (2 * RF), RF)
                rows[pl.ds(start, RF), :] = value[:, :LANE]
                rows[pl.ds(start + RF, RF), :] = value[:, LANE:]

    def build_group(begin, count, stage):
        for h in range(count):
            plain(begin + h, h, stage)

    def fix_group(begin, count, stage):
        for h in range(count):
            clipped(begin + h, h, stage)

    def use_and_build(begin, stage, count, following):
        got = products(0, begin, RUN, lambda b, h: stage[h])
        build_group(begin + RUN, count, following)
        keep(0, begin, got)
        fix_group(begin + RUN, count, following)

    build_group(0, RUN, stage_a)
    fix_group(0, RUN, stage_a)

    def two_groups(i, carry):
        use_and_build(2 * RUN * i, stage_a, RUN, stage_b)
        use_and_build(2 * RUN * i + RUN, stage_b, RUN, stage_a)
        return carry

    turns = BLOCKS // (2 * RUN) - 1
    lax.fori_loop(0, turns, two_groups, 0)
    begin = 2 * RUN * turns
    rest = BLOCKS - begin - 2 * RUN
    use_and_build(begin, stage_a, RUN, stage_b)
    use_and_build(begin + RUN, stage_b, rest, stage_a)
    keep(0, begin + 2 * RUN, products(0, begin + 2 * RUN, rest, lambda b, h: stage_a[h]))

    for step in range(1, 4):

        def forward(scores, count, g, carry):
            got = products(step, RUN * g, count, lambda b, h: band[b])
            for index in range(scores):
                score(step - 1, g * scores + index)
            keep(step, RUN * g, got)
            return carry

        size = BLOCKS - 2 * REACH * step
        scored = OWN // RUN
        lax.fori_loop(0, scored, functools.partial(forward, CH * GROUP // scored, RUN), 0)
        lax.fori_loop(scored, size // RUN, functools.partial(forward, 0, RUN), 0)
        if size % RUN:
            forward(0, size % RUN, size // RUN, 0)

    def only_score(index, carry):
        score(3, index)
        return carry

    lax.fori_loop(0, CH * GROUP, only_score, 0)
    partial = [jnp.sum(sums[level * PER : (level + 1) * PER, :], axis=0, keepdims=True) for level in range(4)]
    partial.append(jnp.sum(aux_ref[GROUP, AREA_AT:, :], axis=0, keepdims=True) * (1.0 / M))
    partial.append(jnp.zeros((PER - len(partial), LANE), F32))
    partial = jnp.concatenate(partial, axis=0)
    for i in range(loss_ref.shape[0]):
        loss_ref[i] = partial

    gs = xs.at[0]
    for step in range(4):
        first = (3 - step) * REACH
        level = {0: 3, 2: 2, 3: 1}.get(step)
        if step > 0 and level is not None:
            for i in range(CHUNKS):
                at = slice((2 * SIDE + i) * LANE, (2 * SIDE + i + 1) * LANE)
                begin = (level * CHUNKS + i) * RB
                total[:, at] = total[:, at] + slopes[begin : begin + RB, :]
        if step == 0:
            for i in range(CHUNKS):
                at = slice((2 * SIDE + i) * LANE, (2 * SIDE + i + 1) * LANE)
                begin = (level * CHUNKS + i) * RB
                gs[: 2 * RB, at] = parts(slopes[begin : begin + RB, :])
        else:

            def refill(p, carry):
                at = tile_at(p + first + REACH)
                gs[: 2 * RB, at] = parts(total[:, at])
                return carry

            lax.fori_loop(0, BLOCKS - 2 * first, refill, 0)
        total[...] = jnp.zeros_like(total)

        def backward(count, g, carry):
            begin = RUN * g + first
            got = []
            for h in range(count):
                value = lax.dot_general(
                    gs[: 2 * RB, tile_at(begin + h + REACH)],
                    band[begin + h],
                    (((1,), (1,)), ((), ())),
                    preferred_element_type=F32,
                )
                got.append(value[:RB] + value[RB:])
            for t in range(2 * REACH + count):
                pieces = [
                    got[h][:, (t - h) * TILE : (t - h + 1) * TILE] for h in range(count) if 0 <= t - h <= 2 * REACH
                ]
                at = tile_at(begin + t)
                total[:, at] = total[:, at] + functools.reduce(jnp.add, pieces)
            return carry

        size = BLOCKS - 2 * first
        lax.fori_loop(0, size // RUN, functools.partial(backward, RUN), 0)
        if size % RUN:
            backward(size % RUN, size // RUN, 0)

    for i in range(CHUNKS):
        at = 2 * SIDE + i
        center_ref[i] = total[:, at * LANE : (at + 1) * LANE] + slopes[i * RB : (i + 1) * RB, :]
    for i in range(EDGE):
        outl_ref[i] = total[:, (1 + i) * LANE : (2 + i) * LANE]
        far = 2 * (SIDE + OWN) + i
        outr_ref[i] = total[:, far * LANE : (far + 1) * LANE]


def final_body(center_ref, arrl_ref, arrr_ref, sums_ref, send_ref, rows):
    for i in range(CHUNKS):
        value = center_ref[i]
        if i < EDGE:
            value = value + arrl_ref[i]
        if i >= CHUNKS - EDGE:
            value = value + arrr_ref[i - (CHUNKS - EDGE)]
        rows[i * RB : (i + 1) * RB, :] = value
    for x in range(GROUP):
        for c in range(CH):
            for m in range(M):
                start = (m * GROUP + x) * NOTE + c * PER
                send_ref[start : start + PER, :] = rows[pl.ds(x * PER * RB + c * M + m, PER, stride=RB), :]
    sums = sums_ref[0]
    for i in range(1, sums_ref.shape[0]):
        sums = sums + sums_ref[i]
    sums = jnp.sum(sums, axis=1, keepdims=True)
    down = lax.broadcasted_iota(jnp.int32, (PER, LANE), 0)
    across = lax.broadcasted_iota(jnp.int32, (PER, LANE), 1)
    note = jnp.sum(jnp.where(down == across, sums, 0.0), axis=0, keepdims=True)
    slots = send_ref.shape[0] // NOTE
    send_ref[pl.ds(NOTE - 1, slots, stride=NOTE), :] = jnp.broadcast_to(note, (slots, LANE))


def spread_body(recv_ref, weight_ref, losses_ref, out_ref):
    slots = recv_ref.shape[0] // NOTE
    sums = jnp.sum(recv_ref[pl.ds(NOTE - 1, slots, stride=NOTE), :], axis=0, keepdims=True)
    lane = lax.broadcasted_iota(jnp.int32, (1, LANE), 1)
    area = jnp.sum(jnp.where(lane == 4, sums, 0.0), axis=1, keepdims=True)
    scale = 1.0 / (jnp.sum(weight_ref[...], axis=1, keepdims=True) * area)
    losses = sums * scale
    for level in range(losses_ref.shape[0]):
        losses_ref[level] = losses[0, level]
    used = out_ref.shape[0] // (CH * PER)
    for c in range(CH):
        for q in range(used):
            part = recv_ref[q * NOTE + c * PER : q * NOTE + (c + 1) * PER, :]
            out_ref[(c * used + q) * PER : (c * used + q + 1) * PER, :] = part * scale


def local(preds, target, area, channel_weight, neighbours):
    members = lax.axis_size("member")
    cells = lax.axis_size("cell")
    channels = preds.shape[1]
    member = lax.axis_index("member")
    cell = lax.axis_index("cell")
    slots = members * GROUP
    used = channels // CH
    rows = range(cells // GROUP)

    by_row = [[m * cells + y * GROUP + x for m in range(members) for x in range(GROUP)] for y in rows]

    def among_rows(move):
        return [(y * GROUP + x, move(y) * GROUP + x) for y in rows if move(y) in rows for x in range(GROUP)]

    def among_four(move):
        return [(y * GROUP + x, y * GROUP + move(x)) for y in rows for x in range(GROUP)]

    def exchange(to_left, to_right):
        return (
            lax.ppermute(to_right, "cell", among_rows(lambda y: y + 1)),
            lax.ppermute(to_left, "cell", among_rows(lambda y: y - 1)),
        )

    place = jnp.stack([cell // GROUP, cell % GROUP]).astype(jnp.int32)
    (send,) = call(pack_body, "pack", [shape(slots * CH * PER, LANE)])(preds)
    send, target, neighbours, area = lax.optimization_barrier((send, target, neighbours, area))
    recv = lax.all_to_all(
        send.reshape(slots, CH * PER, LANE), ("member", "cell"), 0, 0, axis_index_groups=by_row, tiled=True
    )

    by_slot = jnp.pad(target.astype(F32).reshape(CH, used, BLOCK), ((0, 0), (0, slots - used), (0, 0)))
    some = lax.dynamic_slice_in_dim(by_slot, member * GROUP, GROUP, 1)
    some = jnp.moveaxis(some, 1, 0).reshape(GROUP, CH * PER, LANE)
    common = jnp.concatenate([neighbours.astype(F32).reshape(NEIGH * PER, LANE), area.reshape(PER, LANE)])
    side = []
    for shift in range(GROUP):
        to = (cell + shift) % GROUP
        piece = jnp.concatenate([lax.dynamic_index_in_dim(some, to, 0, keepdims=False), common])
        if shift:
            piece = lax.ppermute(piece, "cell", among_four(lambda x: (x + shift) % GROUP))
        side.append(piece)
    side = jnp.stack(side)
    slot = member * GROUP + cell % GROUP
    weights = jnp.pad(channel_weight.reshape(CH, used), ((0, 0), (0, slots - used)))
    weights = lax.dynamic_index_in_dim(weights, slot, 1, keepdims=False)

    own, to_left, to_right = call(
        unpack_body,
        "unpack",
        [shape(CHUNKS, RF, LANE), shape(WIRE, LANE), shape(WIRE, LANE)],
        [pltpu.VMEM((CHUNKS * RF, LANE), F32), pltpu.VMEM((CHUNKS * RT + 16, LANE), F32)],
        scalars=1,
        vectors=2,
    )(place, recv, side)
    own, side, to_left, to_right = lax.optimization_barrier((own, side, to_left, to_right))
    left, right = exchange(to_left, to_right)
    before, after = exchange(side, side)
    aux = jnp.concatenate([before, side, after])

    center, out_left, out_right, sums = call(
        functools.partial(main_body, cells * BLOCK),
        "smooth_score_back",
        [shape(CHUNKS, RB, LANE), shape(EDGE, RB, LANE), shape(EDGE, RB, LANE), shape(len(rows), PER, LANE)],
        [
            pltpu.VMEM((BLOCKS, BAND, TILE), BF16),
            pltpu.VMEM((2, 2 * RF, EXT), BF16),
            pltpu.VMEM((4 * 2 * BLOCKS * RF, LANE), F32),
            pltpu.VMEM((4 * CHUNKS * RB, LANE), F32),
            pltpu.VMEM((RB, EXT), F32),
            pltpu.VMEM((4 * PER, LANE), F32),
            pltpu.VMEM((RUN, BAND, TILE), BF16),
            pltpu.VMEM((RUN, BAND, TILE), BF16),
            pltpu.VMEM((BAND, TILE), BF16),
        ],
        scalars=2,
        vectors=4,
        limit=58,
    )(place, weights, own, left, right, aux)

    arrived = exchange(out_left, out_right)
    by_column = [[y * GROUP + x for y in rows] for x in range(GROUP)]
    sums = lax.all_to_all(sums, "cell", 0, 0, axis_index_groups=by_column, tiled=True)

    (packed,) = call(
        final_body,
        "gather_grad",
        [shape(slots * NOTE, LANE)],
        [pltpu.VMEM((CHUNKS * RB, LANE), F32)],
        vectors=4,
    )(center, *arrived, sums)
    back = lax.all_to_all(
        packed.reshape(slots, 1, NOTE * LANE), ("member", "cell"), 0, 0, axis_index_groups=by_row, tiled=True
    )
    losses, grad = pl.pallas_call(
        spread_body,
        in_specs=[VMEM_SPEC] * 2,
        out_specs=[SMEM_SPEC, VMEM_SPEC],
        out_shape=[shape(4), shape(channels * PER, LANE)],
        compiler_params=pltpu.CompilerParams(vmem_limit_bytes=24 * 1024 * 1024),
        name="spread",
    )(back.reshape(slots * NOTE, LANE), jnp.pad(channel_weight, (0, LANE - channels)).reshape(1, LANE))
    return losses, grad.reshape(1, channels, BLOCK)


def solution(mesh):
    in_specs = (P("member", None, "cell"), P(None, "cell"), P("cell"), P(), P(None, "cell"))
    out_specs = (P(), P("member", None, "cell"))
    return jax.shard_map(local, mesh=mesh, in_specs=in_specs, out_specs=out_specs, check_vma=False)
```

```python
import functools

import jax
import jax.numpy as jnp
from jax import lax
from jax.experimental import pallas as pl
from jax.experimental.pallas import tpu as pltpu
from jax.sharding import PartitionSpec as P

GROUP = 4
CH = 2
M = 16
LANE = 128
NEIGH = 4
ROW = 720
BLOCK = 1024
PER = BLOCK // LANE
WIDTH = GROUP * BLOCK
CHUNKS = WIDTH // LANE
TILE = 256
REACH = 3
BAND = (2 * REACH + 1) * TILE
SIDE = 4 * REACH
OWN = WIDTH // TILE
EXT = (OWN + 2 * SIDE) * TILE
BLOCKS = OWN + 2 * SIDE - 2 * REACH
EDGE = 2 * SIDE - 1
RUN = 4
FIRST = 2
RF = 40
HIGH = 48
RB = CH * M
SPARE = 4 * CHUNKS * RF
RT = RB + CH
WIRE = -(-(EDGE * RT + RF - RT) // 8) * 8
AUX = (CH + NEIGH + 1) * PER
AREA_AT = (CH + NEIGH) * PER
NOTE = CH * PER + 1
DELTA = 0.1
F32 = jnp.float32
BF16 = jnp.bfloat16
SMEM_SPEC = pl.BlockSpec(memory_space=pltpu.SMEM)
VMEM_SPEC = pl.BlockSpec(memory_space=pltpu.VMEM)


def shape(*dims, dtype=F32):
    return jax.ShapeDtypeStruct(dims, dtype)


def call(body, name, outs, scratch=(), scalars=0, vectors=1, limit=24):
    return pl.pallas_call(
        body,
        in_specs=[SMEM_SPEC] * scalars + [VMEM_SPEC] * vectors,
        out_specs=[VMEM_SPEC] * len(outs),
        out_shape=outs,
        scratch_shapes=list(scratch),
        compiler_params=pltpu.CompilerParams(vmem_limit_bytes=limit * 1024 * 1024),
        name=name,
    )


def pack_body(preds_ref, send_ref):
    used = preds_ref.shape[1] // CH
    size = CH * PER
    send_ref[used * size :, :] = jnp.zeros((send_ref.shape[0] - used * size, LANE), F32)
    for c in range(CH):
        for l in range(PER):
            part = preds_ref[0, c * used : (c + 1) * used, l * LANE : (l + 1) * LANE].astype(F32)
            send_ref[pl.ds(c * PER + l, used, stride=size), :] = part


def shift_of(x, mine):
    return (mine - x + GROUP) % GROUP


def unpack_body(place_ref, recv_ref, side_ref, own_ref, left_ref, right_ref, rows, tight):
    rows[...] = jnp.zeros_like(rows)
    tight[...] = jnp.zeros_like(tight)
    for x in range(GROUP):
        for r in range(RT):
            if r < RB:
                c, m = divmod(r, M)
                value = recv_ref[m * GROUP + x, c * PER : (c + 1) * PER, :]
            else:
                c = r - RB
                value = side_ref[shift_of(x, place_ref[1]), c * PER : (c + 1) * PER, :]
            rows[pl.ds(x * PER * RF + r, PER, stride=RF), :] = value
            tight[pl.ds(x * PER * RT + r, PER, stride=RT), :] = value
    for i in range(CHUNKS):
        own_ref[i] = rows[i * RF : (i + 1) * RF, :]
    left_ref[...] = tight[:WIRE, :]
    start = (CHUNKS - EDGE) * RT
    right_ref[...] = tight[start : start + WIRE, :]


def parts(value):
    high = value.astype(BF16).astype(F32)
    return jnp.concatenate([high, value - high], axis=0).astype(BF16)


def tile_at(index, count=1):
    return pl.ds(pl.multiple_of(index * TILE, TILE), count * TILE)


def builder(row_group, mine, aux_ref, band, pattern, cells):
    down = lax.broadcasted_iota(jnp.int32, (TILE, TILE), 0).astype(F32)
    across = lax.broadcasted_iota(jnp.int32, (1, TILE), 1).astype(F32)
    share = 0.5 / NEIGH
    first_cell = row_group * WIDTH - SIDE * TILE
    own = REACH * TILE
    fixed = (own - ROW, own + ROW)

    def hits(place, t):
        return jnp.where(down == place - float(t * TILE), share, 0.0)

    for t in range(2 * REACH + 1):
        total = hits(across + float(fixed[0]), t) + hits(across + float(fixed[1]), t)
        if t == REACH:
            total = total + NEIGH * hits(across + float(own), t)
        pattern[t * TILE : (t + 1) * TILE, :] = total.astype(BF16)

    def places(b, k):
        halves = []
        for h in range(2):
            chunk = CHUNKS - 2 * SIDE + 2 * (b + REACH) + h
            x = (chunk % CHUNKS) // PER
            piece = (chunk // CHUNKS) * GROUP + shift_of(x, mine)
            halves.append(aux_ref[piece, pl.ds(k * PER + chunk % PER, 1), :])
        return jnp.concatenate(halves, axis=1) - (first_cell + b * TILE).astype(F32)

    def plain(b, h, stage):
        near, far = [], []
        for k in (2, 3):
            place = places(b, k)
            high = jnp.floor(place * (1.0 / LANE))
            near.append(jnp.where(down[:LANE] == place - high * LANE, share, 0.0).astype(BF16))
            far.append(high)
        for t in range(BAND // LANE):
            span = slice(t * LANE, (t + 1) * LANE)
            total = pattern[span, :]
            for k in range(2):
                total = total + near[k] * jnp.where(far[k] == float(t), 1.0, 0.0).astype(BF16)
            stage[h, span, :] = total
            band[b, span, :] = total

    def clipped(b, h, stage):
        cell = first_cell + (b + REACH) * TILE

        def correct(k):
            place = places(b, k)
            for t in range(2 * REACH + 1):
                span = slice(t * TILE, (t + 1) * TILE)
                change = hits(place, t) - hits(across + float(fixed[k]), t)
                total = band[b, span, :] + change.astype(BF16)
                stage[h, span, :] = total
                band[b, span, :] = total

        @pl.when((cell >= 0) & (cell < ROW))
        def _():
            correct(0)

        @pl.when((cell < cells) & (cell + TILE > cells - ROW))
        def _():
            correct(1)

    return plain, clipped


def scorer(weight_ref, mine, side_ref, rows, slopes, sums):
    square = DELTA * DELTA
    sums[...] = jnp.zeros_like(sums)

    def one(level, index):
        c = index // GROUP
        x = index % GROUP
        base = (level * CHUNKS + x * PER) * RF
        fields = [rows[pl.ds(base + c * M + m, PER, stride=RF), :] for m in range(M)]
        truth = rows[pl.ds(base + RB + c, PER, stride=RF), :]
        coef = side_ref[shift_of(x, mine), AREA_AT:, :] * weight_ref[c]
        slope = [None] * M
        inverse = jnp.zeros((PER, LANE), F32)
        for a in range(M):
            for b in range(a + 1, M):
                diff = fields[a] - fields[b]
                r = lax.rsqrt(diff * diff + square)
                s = diff * r
                inverse = inverse + r
                slope[a] = s if slope[a] is None else slope[a] + s
                slope[b] = -s if slope[b] is None else slope[b] - s
        pair = square * inverse
        direct_sum = jnp.zeros((PER, LANE), F32)
        out = (level * CHUNKS + x * PER) * RB + c * M
        for m in range(M):
            direct = fields[m] - truth
            q = direct * direct + square
            r = lax.rsqrt(q)
            direct_sum = direct_sum + q * r
            pair = pair + direct * slope[m]
            slopes[pl.ds(out + m, PER, stride=RB), :] = coef * (
                direct * r * (1.0 / M) - slope[m] * (1.0 / (M * (M - 1)))
            )
        term = direct_sum * (1.0 / M) - pair * (1.0 / (M * (M - 1))) - 0.5 * DELTA
        span = slice(level * PER, (level + 1) * PER)
        sums[span, :] = sums[span, :] + coef * term

    return one


def main_body(
    cells, place_ref, weight_ref, own_ref, left_ref, right_ref, side_ref, aux_ref,
    center_ref, outl_ref, outr_ref, loss_ref, band, xs, rows, slopes, total, sums, stage_a, stage_b, pattern,
):
    row_group = place_ref[0]
    mine = place_ref[1]
    plain, clipped = builder(row_group, mine, aux_ref, band, pattern, cells)
    score = scorer(weight_ref, mine, side_ref, rows, slopes, sums)

    xs[0, :, :LANE] = jnp.zeros((2 * RF, LANE), BF16)
    xs[0, :, EXT - LANE :] = jnp.zeros((2 * RF, LANE), BF16)
    for i in range(EDGE):
        near = slice(i * RT, i * RT + RF)
        xs[0, :, (1 + i) * LANE : (2 + i) * LANE] = parts(left_ref[near, :])
        far = 2 * (SIDE + OWN) + i
        xs[0, :, far * LANE : (far + 1) * LANE] = parts(right_ref[near, :])
    for i in range(CHUNKS):
        value = own_ref[i]
        at = 2 * SIDE + i
        xs[0, :, at * LANE : (at + 1) * LANE] = parts(value)
        rows[i * RF : (i + 1) * RF, :] = value

    def products(step, begin, count, read):
        used = HIGH if step == 0 else 2 * RF
        got = []
        for h in range(count):
            b = begin + h + step * REACH
            field = xs[step % 2, :used, tile_at(b, 2 * REACH + 1)]
            got.append(jnp.dot(field, read(b, h), preferred_element_type=F32))
        return got

    def keep(step, begin, got):
        kept = {0: 1, 1: 2, 3: 3}.get(step)
        for h, value in enumerate(got):
            b = begin + h + step * REACH
            value = value[:RF] if step == 0 else value[:RF] + value[RF:]
            if step < 3:
                xs[(step + 1) % 2, :, tile_at(b + REACH)] = parts(value)
            if kept is not None:
                place = b - (SIDE - REACH)
                mine = (place >= 0) & (place < OWN)
                start = jnp.where(mine, kept * (CHUNKS * RF) + place * (2 * RF), SPARE)
                start = pl.multiple_of(start, RF)
                rows[pl.ds(start, RF), :] = value[:, :LANE]
                rows[pl.ds(start + RF, RF), :] = value[:, LANE:]

    def build_group(begin, count, stage):
        for h in range(count):
            plain(begin + h, h, stage)

    def fix_group(begin, count, stage):
        for h in range(count):
            clipped(begin + h, h, stage)

    def use_and_build(begin, stage, count, following):
        got = products(0, begin, FIRST, lambda b, h: stage[h])
        build_group(begin + FIRST, count, following)
        keep(0, begin, got)
        fix_group(begin + FIRST, count, following)

    build_group(0, FIRST, stage_a)
    fix_group(0, FIRST, stage_a)

    def two_groups(i, carry):
        use_and_build(2 * FIRST * i, stage_a, FIRST, stage_b)
        use_and_build(2 * FIRST * i + FIRST, stage_b, FIRST, stage_a)
        return carry

    turns = BLOCKS // (2 * FIRST) - 1
    lax.fori_loop(0, turns, two_groups, 0)
    begin = 2 * FIRST * turns
    rest = BLOCKS - begin - 2 * FIRST
    use_and_build(begin, stage_a, FIRST, stage_b)
    use_and_build(begin + FIRST, stage_b, rest, stage_a)
    keep(0, begin + 2 * FIRST, products(0, begin + 2 * FIRST, rest, lambda b, h: stage_a[h]))

    for step in range(1, 4):

        def forward(scores, count, g, carry):
            got = products(step, RUN * g, count, lambda b, h: band[b])
            for index in range(scores):
                score(step - 1, g * scores + index)
            keep(step, RUN * g, got)
            return carry

        size = BLOCKS - 2 * REACH * step
        scored = OWN // RUN
        lax.fori_loop(0, scored, functools.partial(forward, CH * GROUP // scored, RUN), 0)
        lax.fori_loop(scored, size // RUN, functools.partial(forward, 0, RUN), 0)
        if size % RUN:
            forward(0, size % RUN, size // RUN, 0)

    def only_score(index, carry):
        score(3, index)
        return carry

    lax.fori_loop(0, CH * GROUP, only_score, 0)
    partial = [jnp.sum(sums[level * PER : (level + 1) * PER, :], axis=0, keepdims=True) for level in range(4)]
    partial.append(jnp.sum(side_ref[0, AREA_AT:, :], axis=0, keepdims=True) * (1.0 / M))
    partial.append(jnp.zeros((PER - len(partial), LANE), F32))
    partial = jnp.concatenate(partial, axis=0)
    for i in range(loss_ref.shape[0]):
        loss_ref[i] = partial

    gs = xs.at[0]
    for step in range(4):
        first = (3 - step) * REACH
        level = {0: 3, 2: 2, 3: 1}.get(step)
        if step > 0 and level is not None:
            for i in range(CHUNKS):
                at = slice((2 * SIDE + i) * LANE, (2 * SIDE + i + 1) * LANE)
                begin = (level * CHUNKS + i) * RB
                total[:, at] = total[:, at] + slopes[begin : begin + RB, :]
        if step == 0:
            for i in range(CHUNKS):
                at = slice((2 * SIDE + i) * LANE, (2 * SIDE + i + 1) * LANE)
                begin = (level * CHUNKS + i) * RB
                gs[: 2 * RB, at] = parts(slopes[begin : begin + RB, :])
        else:

            def refill(p, carry):
                at = tile_at(p + first + REACH)
                gs[: 2 * RB, at] = parts(total[:, at])
                return carry

            lax.fori_loop(0, BLOCKS - 2 * first, refill, 0)
        total[...] = jnp.zeros_like(total)

        def backward(count, g, carry):
            begin = RUN * g + first
            got = []
            for h in range(count):
                value = lax.dot_general(
                    gs[: 2 * RB, tile_at(begin + h + REACH)],
                    band[begin + h],
                    (((1,), (1,)), ((), ())),
                    preferred_element_type=F32,
                )
                got.append(value[:RB] + value[RB:])
            for t in range(2 * REACH + count):
                pieces = [
                    got[h][:, (t - h) * TILE : (t - h + 1) * TILE] for h in range(count) if 0 <= t - h <= 2 * REACH
                ]
                at = tile_at(begin + t)
                total[:, at] = total[:, at] + functools.reduce(jnp.add, pieces)
            return carry

        size = BLOCKS - 2 * first
        lax.fori_loop(0, size // RUN, functools.partial(backward, RUN), 0)
        if size % RUN:
            backward(size % RUN, size // RUN, 0)

    for i in range(CHUNKS):
        at = 2 * SIDE + i
        center_ref[i] = total[:, at * LANE : (at + 1) * LANE] + slopes[i * RB : (i + 1) * RB, :]
    for i in range(EDGE):
        outl_ref[i] = total[:, (1 + i) * LANE : (2 + i) * LANE]
        far = 2 * (SIDE + OWN) + i
        outr_ref[i] = total[:, far * LANE : (far + 1) * LANE]


def final_body(center_ref, arrl_ref, arrr_ref, sums_ref, send_ref, rows):
    for i in range(CHUNKS):
        value = center_ref[i]
        if i < EDGE:
            value = value + arrl_ref[i]
        if i >= CHUNKS - EDGE:
            value = value + arrr_ref[i - (CHUNKS - EDGE)]
        rows[i * RB : (i + 1) * RB, :] = value
    for x in range(GROUP):
        for c in range(CH):
            for m in range(M):
                start = (m * GROUP + x) * NOTE + c * PER
                send_ref[start : start + PER, :] = rows[pl.ds(x * PER * RB + c * M + m, PER, stride=RB), :]
    sums = sums_ref[0]
    for i in range(1, sums_ref.shape[0]):
        sums = sums + sums_ref[i]
    sums = jnp.sum(sums, axis=1, keepdims=True)
    down = lax.broadcasted_iota(jnp.int32, (PER, LANE), 0)
    across = lax.broadcasted_iota(jnp.int32, (PER, LANE), 1)
    note = jnp.sum(jnp.where(down == across, sums, 0.0), axis=0, keepdims=True)
    slots = send_ref.shape[0] // NOTE
    send_ref[pl.ds(NOTE - 1, slots, stride=NOTE), :] = jnp.broadcast_to(note, (slots, LANE))


def spread_body(recv_ref, weight_ref, losses_ref, out_ref):
    slots = recv_ref.shape[0] // NOTE
    sums = jnp.sum(recv_ref[pl.ds(NOTE - 1, slots, stride=NOTE), :], axis=0, keepdims=True)
    lane = lax.broadcasted_iota(jnp.int32, (1, LANE), 1)
    area = jnp.sum(jnp.where(lane == 4, sums, 0.0), axis=1, keepdims=True)
    scale = 1.0 / (jnp.sum(weight_ref[...], axis=1, keepdims=True) * area)
    losses = sums * scale
    for level in range(losses_ref.shape[0]):
        losses_ref[level] = losses[0, level]
    used = out_ref.shape[0] // (CH * PER)
    for c in range(CH):
        for q in range(used):
            part = recv_ref[q * NOTE + c * PER : q * NOTE + (c + 1) * PER, :]
            out_ref[(c * used + q) * PER : (c * used + q + 1) * PER, :] = part * scale


def local(preds, target, area, channel_weight, neighbours):
    members = lax.axis_size("member")
    cells = lax.axis_size("cell")
    channels = preds.shape[1]
    member = lax.axis_index("member")
    cell = lax.axis_index("cell")
    slots = members * GROUP
    used = channels // CH
    rows = range(cells // GROUP)

    by_row = [[m * cells + y * GROUP + x for m in range(members) for x in range(GROUP)] for y in rows]

    def among_rows(move):
        return [(y * GROUP + x, move(y) * GROUP + x) for y in rows if move(y) in rows for x in range(GROUP)]

    def among_four(move):
        return [(y * GROUP + x, y * GROUP + move(x)) for y in rows for x in range(GROUP)]

    def exchange(to_left, to_right):
        return (
            lax.ppermute(to_right, "cell", among_rows(lambda y: y + 1)),
            lax.ppermute(to_left, "cell", among_rows(lambda y: y - 1)),
        )

    place = jnp.stack([cell // GROUP, cell % GROUP]).astype(jnp.int32)
    (send,) = call(pack_body, "pack", [shape(slots * CH * PER, LANE)])(preds)
    send, target, neighbours, area = lax.optimization_barrier((send, target, neighbours, area))
    recv = lax.all_to_all(
        send.reshape(slots, CH * PER, LANE), ("member", "cell"), 0, 0, axis_index_groups=by_row, tiled=True
    )

    by_slot = jnp.pad(target.astype(F32).reshape(CH, used, BLOCK), ((0, 0), (0, slots - used), (0, 0)))
    some = lax.dynamic_slice_in_dim(by_slot, member * GROUP, GROUP, 1)
    some = jnp.moveaxis(some, 1, 0).reshape(GROUP, CH * PER, LANE)
    common = jnp.concatenate([neighbours.astype(F32).reshape(NEIGH * PER, LANE), area.reshape(PER, LANE)])
    side = []
    for shift in range(GROUP):
        to = (cell + shift) % GROUP
        piece = jnp.concatenate([lax.dynamic_index_in_dim(some, to, 0, keepdims=False), common])
        if shift:
            piece = lax.ppermute(piece, "cell", among_four(lambda x: (x + shift) % GROUP))
        side.append(piece)
    side = jnp.stack(side)
    slot = member * GROUP + cell % GROUP
    weights = jnp.pad(channel_weight.reshape(CH, used), ((0, 0), (0, slots - used)))
    weights = lax.dynamic_index_in_dim(weights, slot, 1, keepdims=False)

    own, to_left, to_right = call(
        unpack_body,
        "unpack",
        [shape(CHUNKS, RF, LANE), shape(WIRE, LANE), shape(WIRE, LANE)],
        [pltpu.VMEM((CHUNKS * RF, LANE), F32), pltpu.VMEM((CHUNKS * RT + 16, LANE), F32)],
        scalars=1,
        vectors=2,
    )(place, recv, side)
    own, side, to_left, to_right = lax.optimization_barrier((own, side, to_left, to_right))
    left, right = exchange(to_left, to_right)
    index = side[:, CH * PER : AREA_AT, :]
    before, after = exchange(index, index)
    aux = jnp.concatenate([before, index, after])

    center, out_left, out_right, sums = call(
        functools.partial(main_body, cells * BLOCK),
        "smooth_score_back",
        [shape(CHUNKS, RB, LANE), shape(EDGE, RB, LANE), shape(EDGE, RB, LANE), shape(len(rows), PER, LANE)],
        [
            pltpu.VMEM((BLOCKS, BAND, TILE), BF16),
            pltpu.VMEM((2, 2 * RF, EXT), BF16),
            pltpu.VMEM((SPARE + 2 * RF, LANE), F32),
            pltpu.VMEM((4 * CHUNKS * RB, LANE), F32),
            pltpu.VMEM((RB, EXT), F32),
            pltpu.VMEM((4 * PER, LANE), F32),
            pltpu.VMEM((FIRST, BAND, TILE), BF16),
            pltpu.VMEM((FIRST, BAND, TILE), BF16),
            pltpu.VMEM((BAND, TILE), BF16),
        ],
        scalars=2,
        vectors=5,
        limit=48,
    )(place, weights, own, left, right, side, aux)

    arrived = exchange(out_left, out_right)
    by_column = [[y * GROUP + x for y in rows] for x in range(GROUP)]
    sums = lax.all_to_all(sums, "cell", 0, 0, axis_index_groups=by_column, tiled=True)

    (packed,) = call(
        final_body,
        "gather_grad",
        [shape(slots * NOTE, LANE)],
        [pltpu.VMEM((CHUNKS * RB, LANE), F32)],
        vectors=4,
    )(center, *arrived, sums)
    back = lax.all_to_all(
        packed.reshape(slots, 1, NOTE * LANE), ("member", "cell"), 0, 0, axis_index_groups=by_row, tiled=True
    )
    losses, grad = pl.pallas_call(
        spread_body,
        in_specs=[VMEM_SPEC] * 2,
        out_specs=[SMEM_SPEC, VMEM_SPEC],
        out_shape=[shape(4), shape(channels * PER, LANE)],
        compiler_params=pltpu.CompilerParams(vmem_limit_bytes=24 * 1024 * 1024),
        name="spread",
    )(back.reshape(slots * NOTE, LANE), jnp.pad(channel_weight, (0, LANE - channels)).reshape(1, LANE))
    return losses, grad.reshape(1, channels, BLOCK)


def solution(mesh):
    in_specs = (P("member", None, "cell"), P(None, "cell"), P("cell"), P(), P(None, "cell"))
    out_specs = (P(), P("member", None, "cell"))
    return jax.shard_map(local, mesh=mesh, in_specs=in_specs, out_specs=out_specs, check_vma=False)
```
